512 devices in a mesh: grid: 128 (over x, y_hi, z), freq: 4 (over y_lo, core).
Axes of the slice: x: 4, y: 4 (y_hi: 2, y_lo: 2; y = y_hi * 2 + y_lo), z: 16, core: 2. Of those that a mesh axis runs over, the one named last changes fastest.
Arguments:
- amplitude: bfloat16 [16384, 2048], P('grid', 'freq'), may hold values from 0.5 to 1.5
- spectrum: float32 [2048], P('freq'), may hold values from 0.3 to 3
- freq_index: int32 [2, 2048], P(None, 'freq'), may hold values from -128 to 128
- star_offsets: int32 [9, 2], replicated, may hold values from -8 to 8
- valid_mask: int32 [16384], P('grid'), may hold values 0 or 1
Outputs:
- covariance: bfloat16 [128, 2048, 1024], P('grid', 'freq')
The draws below stay inside these ranges and needn't reach their ends.
All inputs are finite; a program needn't handle non-finite values. No bound on the sum of `valid_mask` on one device may be relied on, other than what follows from the above.
Results may differ from the reference program's by a relative error of at most 0.013.
Values may be sent and summed in bfloat16 or wider, within the bound.
A program may use at most 64 MiB of HBM per device.

```python
import math
import jax
import jax.numpy as jnp
from jax import lax

PANEL = 128
FREQ_DEV = 512
NGS = 9
SIDE = 64
NS = 16384
F = 2048
RG = 16
CG = 8
N_GRID = 128
N_FREQ = 4


def touch_ends(array, stream_key, low, high):
    place = [jax.random.randint(jax.random.fold_in(stream_key, axis), (), 0, length) for axis, length in enumerate(array.shape)]
    widest = array.shape.index(max(array.shape))
    next_to = place[:widest] + [(place[widest] + 1) % array.shape[widest]] + place[widest + 1:]
    return array.at[tuple(place)].set(low).at[tuple(next_to)].set(high)


def block_scale(rng, extent, split, low, top_value):
    def one(dim, shards_of):
        heights = jax.random.uniform(jax.random.fold_in(jax.random.fold_in(rng, 6), dim), (shards_of,), jnp.float32, low / len(split), top_value / len(split))
        return jnp.repeat(jnp.exp(heights), extent[dim] // shards_of).reshape((-1,) + (1,) * (len(extent) - dim - 1))

    gain = one(*split[0])
    for cut in split[1:]:
        gain = gain * one(*cut)
    return gain


def setup_inputs(seed: int = 0) -> dict:
    splits = jax.random.split(jax.random.key(seed), 6)
    amplitude = jnp.clip(0.5 + 1.0 * jax.random.uniform(splits[0], (NS, F), jnp.float32) ** block_scale(splits[0], (NS, F), ((0, 128), (1, 4)), -0.2, 0.2), 0.5, 1.5).astype(jnp.bfloat16)
    spectrum = jnp.clip(jnp.exp(math.log(3.0) - 2.3025851 * jax.random.uniform(splits[1], (F,), jnp.float32) ** block_scale(splits[1], (F,), ((0, 4),), -0.2, 0.2)), 0.3, 3.0)
    freq_index = touch_ends(jax.random.randint(splits[2], (2, F), -128, 129), jax.random.fold_in(splits[2], 1), -128, 128).astype(jnp.int32)
    star_offsets = touch_ends(jax.random.randint(splits[3], (NGS, 2), -8, 9), jax.random.fold_in(splits[3], 1), -8, 8).astype(jnp.int32)
    valid_mask = touch_ends((jax.random.randint(splits[4], (NS,), 0, 10) < 9).astype(jnp.int32), jax.random.fold_in(splits[4], 1), 0, 1)
    return {"amplitude": amplitude, "spectrum": spectrum, "freq_index": freq_index, "star_offsets": star_offsets, "valid_mask": valid_mask}


def build_operands(amplitude, spectrum, freq_index, star_offsets, valid_mask):
    slope_count = amplitude.shape[0]
    slope_index = jnp.arange(slope_count, dtype=jnp.int32)
    star_index = slope_index * NGS // slope_count
    subaperture = slope_index // 2
    across = subaperture % SIDE
    upward = subaperture // SIDE % SIDE
    shift_x = star_offsets[star_index, 0]
    shift_y = star_offsets[star_index, 1]
    phase_index = jnp.mod(freq_index[0][None, :] * (2 * across + shift_x)[:, None] + freq_index[1][None, :] * (2 * upward + shift_y)[:, None], 512)
    angles = phase_index.astype(jnp.float32) * (2.0 * math.pi / 512.0)
    scaling = valid_mask.astype(jnp.float32)[:, None] * amplitude.astype(jnp.float32) * jnp.sqrt(spectrum / F)[None, :]
    cosines = (scaling * jnp.cos(angles)).astype(jnp.bfloat16)
    sines = (scaling * jnp.sin(angles)).astype(jnp.bfloat16)
    return (cosines, sines)

def reference(amplitude, spectrum, freq_index, star_offsets, valid_mask):
    cosines, sines = build_operands(amplitude, spectrum, freq_index, star_offsets, valid_mask)
    row_span = RG * PANEL

    def one_tile(tile_index):
        row_group = tile_index // RG
        col_group = tile_index % RG
        first = (row_group * row_span).astype(jnp.int32)
        rows_cos = lax.dynamic_slice_in_dim(cosines, first, row_span, 0)
        rows_sin = lax.dynamic_slice_in_dim(sines, first, row_span, 0)
        cols_cos = lax.dynamic_index_in_dim(cosines.reshape(CG, RG, PANEL, F), col_group, 1, keepdims=False).reshape(CG * PANEL, F)
        cols_sin = lax.dynamic_index_in_dim(sines.reshape(CG, RG, PANEL, F), col_group, 1, keepdims=False).reshape(CG * PANEL, F)
        summed = jnp.zeros((row_span, CG * PANEL), jnp.float32)
        for block in range(N_FREQ):
            low = block * FREQ_DEV
            high = low + FREQ_DEV
            partial_value = jnp.dot(rows_cos[:, low:high], cols_cos[:, low:high].T, preferred_element_type=jnp.float32)
            partial_value = partial_value + jnp.dot(rows_sin[:, low:high], cols_sin[:, low:high].T, preferred_element_type=jnp.float32)
            rounded = lax.optimization_barrier(partial_value.astype(jnp.bfloat16))
            summed = summed + rounded.astype(jnp.float32)
        return summed.astype(jnp.bfloat16)
    return lax.map(one_tile, jnp.arange(N_GRID, dtype=jnp.int32))
```

```python
import math

import jax
import jax.numpy as jnp
from jax import lax
from jax.experimental import pallas as pl
from jax.experimental.pallas import tpu as pltpu
from jax.sharding import PartitionSpec as P

NGS = 9
PANEL = 128
NZ = 16
NX = 4
SUBS = 4
HALF = NZ // 2
MESH = pl.DeviceIdType.MESH


def cos_sin(phase):
    index = phase.astype(jnp.int32) & 511
    quadrant = (index + 64) >> 7
    x = (index - (quadrant << 7)).astype(jnp.float32) * (2.0 * math.pi / 512.0)
    y = x * x
    sin = x * (1.0 + y * (-1 / 6 + y * (1 / 120 + y * (-1 / 5040 + y * (1 / 362880)))))
    cos = 1.0 + y * (-0.5 + y * (1 / 24 + y * (-1 / 720 + y * (1 / 40320 + y * (-1 / 3628800)))))
    swap = (quadrant & 1) == 1
    cos, sin = jnp.where(swap, sin, cos), jnp.where(swap, cos, sin)
    cos = jnp.where(((quadrant + 1) & 2) != 0, -cos, cos)
    sin = jnp.where((quadrant & 2) != 0, -sin, sin)
    return cos, sin


def kernel(
    amp_ref, spec_ref, freq_ref, star_ref, mask_ref, out_ref,
    rows, cols, rop, cop, pack, base_c, base_s, turn_p, turn_c, turn_s, mask_t, acc,
    zs, zr, hs, hr, ps, pr, ys, yr, xs, xr, fs, fr, ss, sr,
):
    g, f = lax.axis_index("grid"), lax.axis_index("freq")
    z, a = g % NZ, g // NZ
    x, yh = a // 2, a % 2
    yl, core = f // 2, f % 2
    width = amp_ref.shape[1]

    f1 = f + 1 - 2 * core
    f2 = f + 2 - 4 * yl
    f3 = f1 + 2 - 4 * yl
    a_far = a + 1 - 2 * yh
    g_far = a_far * NZ + z

    def at_z(step):
        return a * NZ + (z + step + NZ) % NZ

    def at_x(step):
        return (((x + step + NX) % NX) * 2 + yh) * NZ + z

    barrier = pltpu.get_barrier_semaphore()
    peers = [
        (at_z(1), f), (at_z(-1), f), (g, f1), (g, f2), (g, f3),
        (g_far, f), (g_far, f2), (at_x(1), f), (at_x(-1), f),
    ]
    for peer in peers:
        pl.semaphore_signal(barrier, inc=1, device_id=peer, device_id_type=MESH)

    mask_t[...] = jnp.broadcast_to(mask_ref[...].astype(jnp.float32), (PANEL, PANEL)).T
    for n in range(width // 128):
        lanes = pl.ds(n * 128, 128)
        masked = (amp_ref[:, lanes].astype(jnp.float32) * mask_t[...]).astype(jnp.bfloat16)
        rows[z, f, :, lanes] = masked
        cols[f, a, :, lanes] = masked
    total = width * lax.axis_size("freq")
    pack[f, 0:2, :] = freq_ref[...].astype(jnp.float32)
    pack[f, 2:3, :] = jnp.sqrt(spec_ref[...] / total)

    pl.semaphore_wait(barrier, len(peers))

    started = []

    def send(src, dst, send_sem, recv_sem, peer):
        return pltpu.make_async_remote_copy(
            src_ref=src, dst_ref=dst, send_sem=send_sem, recv_sem=recv_sem,
            device_id=peer, device_id_type=MESH,
        )

    def begin(copy):
        copy.start()
        started.append(copy)

    piece = PANEL // SUBS

    def ring(t, way, sub):
        panel = (z - (1, -1)[way] * (t - 1) + NZ) % NZ
        part = rows.at[panel, f, pl.ds(sub * piece, piece)]
        return send(part, part, zs.at[way, t - 1, sub], zr.at[way, t - 1, sub], (at_z((1, -1)[way]), f))

    def ring_got(t, way, sub):
        panel = (z - (1, -1)[way] * t + NZ) % NZ
        part = rows.at[panel, f, pl.ds(sub * piece, piece)]
        send(part, part, zs.at[way, t - 1, sub], zr.at[way, t - 1, sub], (at_z((1, -1)[way]), f)).wait_recv()

    def ways(t, sub):
        if t < HALF:
            return (0, 1)
        return (0,) if sub < SUBS // 2 else (1,)

    def hand(slot, panel, start):
        owner, place = panel // 4, panel % 4

        @pl.when(owner != f)
        def _():
            copy = send(rows.at[panel, f], rows.at[panel, f], hs.at[slot], hr.at[place, f], (g, owner))
            if start:
                copy.start()
            else:
                copy.wait_send()

    def slots(t):
        if t == 0:
            return [(0, z)]
        if t == HALF:
            return [(2 * HALF - 1, (z + HALF) % NZ)]
        return [(2 * t - 1, (z - t + NZ) % NZ), (2 * t, (z + t) % NZ)]

    def ring_step(t):
        for sub in range(SUBS):
            for way in ways(t, sub):
                ring_got(t, way, sub)
                if t < HALF and way in ways(t + 1, sub):
                    begin(ring(t + 1, way, sub))
        for slot, panel in slots(t):
            hand(slot, panel, True)

    def col_send(panel, q, send_sem, recv_sem, peer):
        return send(cols.at[q, panel], cols.at[q, panel], send_sem, recv_sem, peer)

    def y_copies():
        return [
            col_send(a, f, ys.at[0], yr.at[0], (g_far, f2)),
            col_send(a, f, ys.at[1], yr.at[1], (g, f2)),
            col_send(a, f, ys.at[2], yr.at[2], (g_far, f)),
        ]

    y_items = [(a_far, f2), (a, f2), (a_far, f)]
    quad = [(0, f), (1, f2), (0, f2), (1, f)]

    def col_of(step, other):
        return ((x + step + NX) % NX) * 2 + (yh if other == 0 else 1 - yh)

    def x_copy(n, way):
        other, q = quad[n]
        return col_send(col_of(0, other), q, xs.at[way, n], xr.at[way, n], (at_x((1, -1)[way]), f))

    def x_got(n, way):
        other, q = quad[n]
        panel = col_of(-(1, -1)[way], other)
        col_send(panel, q, xs.at[way, n], xr.at[way, n], (at_x(0), f)).wait_recv()
        return panel, q

    forward = {(0, 0): 0, (0, 3): 1, (1, 1): 0, (1, 2): 1}

    def x_forward(n, way):
        other, q = quad[n]
        panel = col_of(-(1, -1)[way], other)
        return col_send(panel, q, fs.at[way, forward[way, n]], fr.at[way, forward[way, n]], (at_x((1, -1)[way]), f))

    def f_got(way, n):
        other, q = quad[n]
        panel = col_of(2, other)
        col_send(panel, q, fs.at[way, forward[way, n]], fr.at[way, forward[way, n]], (at_x(0), f)).wait_recv()
        return panel, q

    sibling = []

    def share(panel, q):
        n = len(sibling)
        sibling.append((panel, q))
        begin(col_send(panel, q, ss.at[n], sr.at[n], (g, f1)))

    def other_core(q):
        return q + 1 - 2 * core

    def share_got(n):
        panel, q = sibling[n]
        mine = other_core(q)
        col_send(panel, mine, ss.at[n], sr.at[n], (g, f1)).wait_recv()
        return panel, mine

    def base_table(q):
        kx = pack[q, 0:1, :]

        def step(i, carry):
            at = pl.ds(pl.multiple_of(i * 16, 16), 16)
            across = (lax.broadcasted_iota(jnp.int32, (16, width), 0) + i * 16) >> 1
            cos, sin = cos_sin(kx * (2 * across).astype(jnp.float32))
            base_c[q, at, :] = cos
            base_s[q, at, :] = sin
            return carry

        lax.fori_loop(0, PANEL // 16, step, 0)

    slope_count = PANEL * lax.axis_size("grid")
    group = a * NZ + f * 4
    turn_panels = [n * NZ + z for n in range(2 * NX)] + [group + n for n in range(4)]

    def turn_table(q):
        kx, ky = pack[q, 0:1, :], pack[q, 1:2, :]
        for n, panel in enumerate(turn_panels):
            upward = 2 * (panel % 64)
            star = panel * PANEL * NGS // slope_count
            for m in range(2):
                index = jnp.minimum(star + m, NGS - 1)
                turn_x = star_ref[index, 0].astype(jnp.float32)
                turn_y = (star_ref[index, 1] + upward).astype(jnp.float32)
                turn_p[2 * n + m : 2 * n + m + 1, :] = kx * turn_x + ky * turn_y
        weight = pack[q, 2:3, :]
        cos, sin = cos_sin(turn_p[...])
        turn_c[q] = cos * weight
        turn_s[q] = sin * weight

    def build(source, panel, q, turn, into):
        star = panel * PANEL * NGS // slope_count
        bound = ((star + 1) * slope_count + NGS - 1) // NGS - panel * PANEL
        c0, c1 = turn_c[q, pl.ds(2 * turn, 1), :], turn_c[q, pl.ds(2 * turn + 1, 1), :]
        s0, s1 = turn_s[q, pl.ds(2 * turn, 1), :], turn_s[q, pl.ds(2 * turn + 1, 1), :]

        def step(i, carry):
            at = pl.ds(pl.multiple_of(i * 16, 16), 16)
            first = lax.broadcasted_iota(jnp.int32, (16, width), 0) + i * 16 < bound
            tc, ts = jnp.where(first, c0, c1), jnp.where(first, s0, s1)
            value = source[at, :].astype(jnp.float32)
            bc, bs = base_c[q, at, :], base_s[q, at, :]
            into(i, (value * (bc * tc - bs * ts)).astype(jnp.bfloat16), (value * (bs * tc + bc * ts)).astype(jnp.bfloat16))
            return carry

        lax.fori_loop(0, PANEL // 16, step, 0)

    def build_col(item):
        panel, q = item
        half, part = q // 2, q % 2

        def into(i, cos, sin):
            at = pl.ds(pl.multiple_of(panel * PANEL + i * 16, 16), 16)
            cop[half, at, pl.ds(pl.multiple_of(part * 2 * width, 128), width)] = cos
            cop[half, at, pl.ds(pl.multiple_of(part * 2 * width + width, 128), width)] = sin

        build(cols.at[q, panel], panel * NZ + z, q, panel, into)

    for sub in range(SUBS):
        for way in (0, 1):
            begin(ring(1, way, sub))
    packs = [
        send(pack.at[f], pack.at[f], ps.at[n], pr.at[n], (g, peer)) for n, peer in enumerate((f1, f2, f3))
    ]
    for copy in packs:
        begin(copy)
    for copy in y_copies():
        begin(copy)
    for way in (0, 1):
        begin(x_copy(0, way))
    hand(0, z, True)
    share(a, f)

    base_table(f)
    turn_table(f)
    for n, q in enumerate((f1, f2, f3)):
        send(pack.at[q], pack.at[q], ps.at[n], pr.at[n], (g, q)).wait_recv()
        if n == 0:
            base_table(q)
            turn_table(q)

    ring_step(1)
    base_table(f2)
    turn_table(f2)
    base_table(f3)
    turn_table(f3)

    ring_step(2)
    for n, (panel, q) in enumerate(y_items):
        col_send(panel, q, ys.at[n], yr.at[n], (g, f)).wait_recv()
        for way in (0, 1):
            begin(x_copy(n + 1, way))
        share(panel, q)
    for way in (0, 1):
        item = x_got(0, way)
        if (way, 0) in forward:
            begin(x_forward(0, way))
        share(*item)
    build_col((a, f))
    build_col(share_got(0))

    ring_step(3)
    for n in range(3):
        build_col(y_items[n])
        build_col(share_got(1 + n))

    ring_step(4)
    build_col(sibling[4])
    build_col(sibling[5])
    build_col(share_got(4))
    build_col(share_got(5))

    ring_step(5)
    for way in (0, 1):
        item = x_got(1, way)
        if (way, 1) in forward:
            begin(x_forward(1, way))
        share(*item)
        build_col(item)
    ring_step(6)
    build_col(share_got(6))
    build_col(share_got(7))
    for n in (2, 3):
        for way in (0, 1):
            item = x_got(n, way)
            if (way, n) in forward:
                begin(x_forward(n, way))
            share(*item)
    build_col(sibling[8])
    build_col(sibling[9])

    ring_step(7)
    build_col(sibling[10])
    build_col(sibling[11])
    for n in range(8, 12):
        build_col(share_got(n))

    ring_step(8)
    for way, n in ((0, 0), (1, 1), (1, 2), (0, 3)):
        item = f_got(way, n)
        share(*item)
        build_col(item)
    for n in range(12, 16):
        build_col(share_got(n))

    ahead = (4 * f + 1 - z + NZ) % NZ < HALF

    def unit(n):
        place = jnp.where(ahead, n, 3 - n)
        panel = 4 * f + place
        for near in (True, False):
            half = yl if near else 1 - yl
            for q in ((f1,) if near else (f2, f3)):
                part = rows.at[panel, q]
                send(part, part, hs.at[0], hr.at[place, q], (g, f1)).wait_recv()
            for part in range(2):
                q = half * 2 + part

                def into(i, cos, sin, part=part):
                    at = pl.ds(pl.multiple_of(i * 16, 16), 16)
                    rop[at, 2 * part * width : (2 * part + 1) * width] = cos
                    rop[at, (2 * part + 1) * width : (2 * part + 2) * width] = sin

                build(rows.at[panel, q], a * NZ + panel, q, 2 * NX + place, into)

            def dot(i, carry):
                at = pl.ds(pl.multiple_of(i * 256, 256), 256)
                value = lax.dot_general(
                    rop[...], cop[half, at, :], (((1,), (1,)), ((), ())), preferred_element_type=jnp.float32
                )
                if near:
                    acc[:, at] = value
                else:
                    to = pl.ds(pl.multiple_of(place * PANEL, PANEL), PANEL)
                    out_ref[0, to, at] = (acc[:, at] + value).astype(jnp.bfloat16)
                return carry

            lax.fori_loop(0, cop.shape[1] // 256, dot, 0)

    lax.fori_loop(0, 4, lambda n, carry: (unit(n), carry)[1], 0)

    for copy in started:
        copy.wait_send()
    for t in range(HALF + 1):
        for slot, panel in slots(t):
            hand(slot, panel, False)


def on_device(amplitude, spectrum, freq_index, star_offsets, valid_mask):
    width = amplitude.shape[1]
    vmem = pl.BlockSpec(memory_space=pltpu.VMEM)
    dma = pltpu.SemaphoreType.DMA
    return pl.pallas_call(
        kernel,
        out_shape=jax.ShapeDtypeStruct((1, 4 * PANEL, 2 * NX * PANEL), jnp.bfloat16),
        in_specs=[vmem, vmem, vmem, pl.BlockSpec(memory_space=pltpu.SMEM), vmem],
        out_specs=vmem,
        scratch_shapes=[
            pltpu.VMEM((NZ, 4, PANEL, width), jnp.bfloat16),
            pltpu.VMEM((4, 2 * NX, PANEL, width), jnp.bfloat16),
            pltpu.VMEM((PANEL, 4 * width), jnp.bfloat16),
            pltpu.VMEM((2, 2 * NX * PANEL, 4 * width), jnp.bfloat16),
            pltpu.VMEM((4, 8, width), jnp.float32),
            pltpu.VMEM((4, PANEL, width), jnp.float32),
            pltpu.VMEM((4, PANEL, width), jnp.float32),
            pltpu.VMEM((24, width), jnp.float32),
            pltpu.VMEM((4, 24, width), jnp.float32),
            pltpu.VMEM((4, 24, width), jnp.float32),
            pltpu.VMEM((PANEL, PANEL), jnp.float32),
            pltpu.VMEM((PANEL, 2 * NX * PANEL), jnp.float32),
            dma((2, HALF, SUBS)), dma((2, HALF, SUBS)),
            dma((16,)), dma((4, 4)),
            dma((3,)), dma((3,)),
            dma((3,)), dma((3,)),
            dma((2, 4)), dma((2, 4)),
            dma((2, 2)), dma((2, 2)),
            dma((16,)), dma((16,)),
        ],
        compiler_params=pltpu.CompilerParams(
            collective_id=0, has_side_effects=True, vmem_limit_bytes=56 * 2**20
        ),
        cost_estimate=pl.CostEstimate(flops=2 * 512 * 1024 * 4096, bytes_accessed=2 * 2**20, transcendentals=0),
    )(amplitude, spectrum.reshape(1, width), freq_index, star_offsets, valid_mask.reshape(1, PANEL))


def solution(mesh):
    placed = (P("grid", "freq"), P("freq"), P(None, "freq"), P(), P("grid"))
    return jax.shard_map(
        on_device, mesh=mesh, in_specs=placed, out_specs=P("grid", "freq", None), check_vma=False
    )
```

```python
import math

import jax
import jax.numpy as jnp
from jax import lax
from jax.experimental import pallas as pl
from jax.experimental.pallas import tpu as pltpu
from jax.sharding import PartitionSpec as P

NGS = 9
PANEL = 128
NZ = 16
NX = 4
SUBS = 4
HALF = NZ // 2
MESH = pl.DeviceIdType.MESH


def cos_sin(phase):
    index = phase.astype(jnp.int32) & 511
    quadrant = (index + 64) >> 7
    x = (index - (quadrant << 7)).astype(jnp.float32) * (2.0 * math.pi / 512.0)
    y = x * x
    sin = x * (1.0 + y * (-1 / 6 + y * (1 / 120 + y * (-1 / 5040 + y * (1 / 362880)))))
    cos = 1.0 + y * (-0.5 + y * (1 / 24 + y * (-1 / 720 + y * (1 / 40320 + y * (-1 / 3628800)))))
    swap = (quadrant & 1) == 1
    cos, sin = jnp.where(swap, sin, cos), jnp.where(swap, cos, sin)
    cos = jnp.where(((quadrant + 1) & 2) != 0, -cos, cos)
    sin = jnp.where((quadrant & 2) != 0, -sin, sin)
    return cos, sin


def kernel(
    amp_ref, spec_ref, freq_ref, star_ref, mask_ref, out_ref,
    rows, cols, rop, cop, pack, base_c, base_s, turn_p, turn_c, turn_s, mask_t, acc,
    zs, zr, hs, hr, ps, pr, ys, yr, xs, xr, fs, fr, ss, sr,
):
    g, f = lax.axis_index("grid"), lax.axis_index("freq")
    z, a = g % NZ, g // NZ
    x, yh = a // 2, a % 2
    yl, core = f // 2, f % 2
    width = amp_ref.shape[1]

    f1 = f + 1 - 2 * core
    f2 = f + 2 - 4 * yl
    f3 = f1 + 2 - 4 * yl
    a_far = a + 1 - 2 * yh
    g_far = a_far * NZ + z

    def at_z(step):
        return a * NZ + (z + step + NZ) % NZ

    def at_x(step):
        return (((x + step + NX) % NX) * 2 + yh) * NZ + z

    barrier = pltpu.get_barrier_semaphore()
    peers = [
        (at_z(1), f), (at_z(-1), f), (g, f1), (g, f2), (g, f3),
        (g_far, f), (g_far, f2), (at_x(1), f), (at_x(-1), f),
    ]
    for peer in peers:
        pl.semaphore_signal(barrier, inc=1, device_id=peer, device_id_type=MESH)

    mask_t[...] = jnp.broadcast_to(mask_ref[...].astype(jnp.float32), (PANEL, PANEL)).T
    for n in range(width // 128):
        lanes = pl.ds(n * 128, 128)
        masked = (amp_ref[:, lanes].astype(jnp.float32) * mask_t[...]).astype(jnp.bfloat16)
        rows[z, f, :, lanes] = masked
        cols[f, a, :, lanes] = masked
    total = width * lax.axis_size("freq")
    pack[f, 0:2, :] = freq_ref[...].astype(jnp.float32)
    pack[f, 2:3, :] = jnp.sqrt(spec_ref[...] / total)

    pl.semaphore_wait(barrier, len(peers))

    started = []

    def send(src, dst, send_sem, recv_sem, peer):
        return pltpu.make_async_remote_copy(
            src_ref=src, dst_ref=dst, send_sem=send_sem, recv_sem=recv_sem,
            device_id=peer, device_id_type=MESH,
        )

    def begin(copy):
        copy.start()
        started.append(copy)

    piece = PANEL // SUBS

    def ring(t, way, sub):
        panel = (z - (1, -1)[way] * (t - 1) + NZ) % NZ
        part = rows.at[panel, f, pl.ds(sub * piece, piece)]
        return send(part, part, zs.at[way, t - 1, sub], zr.at[way, t - 1, sub], (at_z((1, -1)[way]), f))

    def ring_got(t, way, sub):
        panel = (z - (1, -1)[way] * t + NZ) % NZ
        part = rows.at[panel, f, pl.ds(sub * piece, piece)]
        send(part, part, zs.at[way, t - 1, sub], zr.at[way, t - 1, sub], (at_z((1, -1)[way]), f)).wait_recv()

    def ways(t, sub):
        if t < HALF:
            return (0, 1)
        return (0,) if sub < SUBS // 2 else (1,)

    def hand(slot, panel, start):
        owner, place = panel // 4, panel % 4

        @pl.when(owner != f)
        def _():
            copy = send(rows.at[panel, f], rows.at[panel, f], hs.at[slot], hr.at[place, f], (g, owner))
            if start:
                copy.start()
            else:
                copy.wait_send()

    def slots(t):
        if t == 0:
            return [(0, z)]
        if t == HALF:
            return [(2 * HALF - 1, (z + HALF) % NZ)]
        return [(2 * t - 1, (z - t + NZ) % NZ), (2 * t, (z + t) % NZ)]

    def ring_step(t):
        for sub in range(SUBS):
            for way in ways(t, sub):
                ring_got(t, way, sub)
                if t < HALF and way in ways(t + 1, sub):
                    begin(ring(t + 1, way, sub))
        for slot, panel in slots(t):
            hand(slot, panel, True)

    def col_send(panel, q, send_sem, recv_sem, peer):
        return send(cols.at[q, panel], cols.at[q, panel], send_sem, recv_sem, peer)

    def y_copies():
        return [
            col_send(a, f, ys.at[0], yr.at[0], (g_far, f2)),
            col_send(a, f, ys.at[1], yr.at[1], (g, f2)),
            col_send(a, f, ys.at[2], yr.at[2], (g_far, f)),
        ]

    y_items = [(a_far, f2), (a, f2), (a_far, f)]
    quad = [(0, f), (1, f2), (0, f2), (1, f)]

    def col_of(step, other):
        return ((x + step + NX) % NX) * 2 + (yh if other == 0 else 1 - yh)

    def x_copy(n, way):
        other, q = quad[n]
        return col_send(col_of(0, other), q, xs.at[way, n], xr.at[way, n], (at_x((1, -1)[way]), f))

    def x_got(n, way):
        other, q = quad[n]
        panel = col_of(-(1, -1)[way], other)
        col_send(panel, q, xs.at[way, n], xr.at[way, n], (at_x(0), f)).wait_recv()
        return panel, q

    forward = {(0, 0): 0, (0, 3): 1, (1, 1): 0, (1, 2): 1}

    def x_forward(n, way):
        other, q = quad[n]
        panel = col_of(-(1, -1)[way], other)
        return col_send(panel, q, fs.at[way, forward[way, n]], fr.at[way, forward[way, n]], (at_x((1, -1)[way]), f))

    def f_got(way, n):
        other, q = quad[n]
        panel = col_of(2, other)
        col_send(panel, q, fs.at[way, forward[way, n]], fr.at[way, forward[way, n]], (at_x(0), f)).wait_recv()
        return panel, q

    sibling = []

    def share(panel, q):
        n = len(sibling)
        sibling.append((panel, q))
        begin(col_send(panel, q, ss.at[n], sr.at[n], (g, f1)))

    def other_core(q):
        return q + 1 - 2 * core

    def share_got(n):
        panel, q = sibling[n]
        mine = other_core(q)
        col_send(panel, mine, ss.at[n], sr.at[n], (g, f1)).wait_recv()
        return panel, mine

    def base_table(q):
        kx = pack[q, 0:1, :]

        def step(i, carry):
            at = pl.ds(pl.multiple_of(i * 16, 16), 16)
            across = (lax.broadcasted_iota(jnp.int32, (16, width), 0) + i * 16) >> 1
            cos, sin = cos_sin(kx * (2 * across).astype(jnp.float32))
            base_c[q, at, :] = cos
            base_s[q, at, :] = sin
            return carry

        lax.fori_loop(0, PANEL // 16, step, 0)

    slope_count = PANEL * lax.axis_size("grid")
    group = a * NZ + f * 4
    turn_panels = [n * NZ + z for n in range(2 * NX)] + [group + n for n in range(4)]

    def turn_table(q):
        kx, ky = pack[q, 0:1, :], pack[q, 1:2, :]
        for n, panel in enumerate(turn_panels):
            upward = 2 * (panel % 64)
            star = panel * PANEL * NGS // slope_count
            for m in range(2):
                index = jnp.minimum(star + m, NGS - 1)
                turn_x = star_ref[0, index].astype(jnp.float32)
                turn_y = (star_ref[1, index] + upward).astype(jnp.float32)
                turn_p[2 * n + m : 2 * n + m + 1, :] = kx * turn_x + ky * turn_y
        weight = pack[q, 2:3, :]
        cos, sin = cos_sin(turn_p[...])
        turn_c[q] = cos * weight
        turn_s[q] = sin * weight

    def build(source, panel, q, turn, into):
        star = panel * PANEL * NGS // slope_count
        bound = ((star + 1) * slope_count + NGS - 1) // NGS - panel * PANEL
        c0, c1 = turn_c[q, pl.ds(2 * turn, 1), :], turn_c[q, pl.ds(2 * turn + 1, 1), :]
        s0, s1 = turn_s[q, pl.ds(2 * turn, 1), :], turn_s[q, pl.ds(2 * turn + 1, 1), :]

        def step(i, carry):
            at = pl.ds(pl.multiple_of(i * 16, 16), 16)
            first = lax.broadcasted_iota(jnp.int32, (16, width), 0) + i * 16 < bound
            tc, ts = jnp.where(first, c0, c1), jnp.where(first, s0, s1)
            value = source[at, :].astype(jnp.float32)
            bc, bs = base_c[q, at, :], base_s[q, at, :]
            into(i, (value * (bc * tc - bs * ts)).astype(jnp.bfloat16), (value * (bs * tc + bc * ts)).astype(jnp.bfloat16))
            return carry

        lax.fori_loop(0, PANEL // 16, step, 0, unroll=8)

    def build_col(item):
        panel, q = item
        half, part = q // 2, q % 2

        def into(i, cos, sin):
            at = pl.ds(pl.multiple_of(panel * PANEL + i * 16, 16), 16)
            cop[half, at, pl.ds(pl.multiple_of(part * 2 * width, 128), width)] = cos
            cop[half, at, pl.ds(pl.multiple_of(part * 2 * width + width, 128), width)] = sin

        build(cols.at[q, panel], panel * NZ + z, q, panel, into)

    ahead = (4 * f + 1 - z + NZ) % NZ < HALF

    def row_operand(place, q):
        panel = 4 * f + place
        part = q % 2

        def into(i, cos, sin):
            at = pl.ds(pl.multiple_of(place * PANEL + i * 16, 16), 16)
            rop[q // 2, at, pl.ds(pl.multiple_of(part * 2 * width, 128), width)] = cos
            rop[q // 2, at, pl.ds(pl.multiple_of(part * 2 * width + width, 128), width)] = sin

        build(rows.at[panel, q], a * NZ + panel, q, 2 * NX + place, into)

    def handed(place, q):
        part = rows.at[4 * f + place, q]
        send(part, part, hs.at[0], hr.at[place, q], (g, f1)).wait_recv()
        row_operand(place, q)

    def own_rows(t, of_core):
        for _, panel in slots(t):
            @pl.when(panel // 4 == f)
            def _():
                if of_core:
                    row_operand(panel % 4, f)
                else:
                    handed(panel % 4, f1)

    def product(m, near):
        half = yl if near else 1 - yl
        at = pl.ds(pl.multiple_of(jnp.where(ahead, 2 * m, 2 - 2 * m) * PANEL, PANEL), 2 * PANEL)

        def dot(i, carry):
            to = pl.ds(pl.multiple_of(i * 512, 512), 512)
            value = lax.dot_general(
                rop[half, at, :], cop[half, to, :], (((1,), (1,)), ((), ())), preferred_element_type=jnp.float32
            )
            if near:
                acc[at, to] = value
            else:
                out_ref[0, at, to] = (acc[at, to] + value).astype(jnp.bfloat16)
            return carry

        lax.fori_loop(0, cop.shape[1] // 512, dot, 0)

    def far_rows(m):
        for n in range(2):
            for q in (f2, f3):
                handed(jnp.where(ahead, 2 * m + n, 3 - 2 * m - n), q)

    for sub in range(SUBS):
        for way in (0, 1):
            begin(ring(1, way, sub))
    packs = [
        send(pack.at[f], pack.at[f], ps.at[n], pr.at[n], (g, peer)) for n, peer in enumerate((f1, f2, f3))
    ]
    for copy in packs:
        begin(copy)
    for copy in y_copies():
        begin(copy)
    for way in (0, 1):
        begin(x_copy(0, way))
    hand(0, z, True)
    share(a, f)

    base_table(f)
    turn_table(f)
    for n, q in enumerate((f1, f2, f3)):
        send(pack.at[q], pack.at[q], ps.at[n], pr.at[n], (g, q)).wait_recv()
        if n == 0:
            base_table(q)
            turn_table(q)

    own_rows(0, True)
    ring_step(1)
    base_table(f2)
    turn_table(f2)
    base_table(f3)
    turn_table(f3)
    own_rows(0, False)
    own_rows(1, True)

    ring_step(2)
    for n, (panel, q) in enumerate(y_items):
        col_send(panel, q, ys.at[n], yr.at[n], (g, f)).wait_recv()
        for way in (0, 1):
            begin(x_copy(n + 1, way))
        share(panel, q)
    for way in (0, 1):
        item = x_got(0, way)
        if (way, 0) in forward:
            begin(x_forward(0, way))
        share(*item)
    build_col((a, f))
    build_col(share_got(0))
    own_rows(1, False)
    own_rows(2, True)

    ring_step(3)
    for n in range(3):
        build_col(y_items[n])
        build_col(share_got(1 + n))
    own_rows(2, False)
    own_rows(3, True)

    ring_step(4)
    for way in (0, 1):
        item = x_got(1, way)
        if (way, 1) in forward:
            begin(x_forward(1, way))
        share(*item)
    for n in (4, 5):
        build_col(sibling[n])
        build_col(share_got(n))
    own_rows(3, False)
    own_rows(4, True)

    ring_step(5)
    for n in (2, 3):
        for way in (0, 1):
            item = x_got(n, way)
            if (way, n) in forward:
                begin(x_forward(n, way))
            share(*item)
    for n in (6, 7):
        build_col(sibling[n])
        build_col(share_got(n))
    own_rows(4, False)
    own_rows(5, True)

    ring_step(6)
    for n in range(8, 12):
        build_col(sibling[n])
        build_col(share_got(n))
    own_rows(5, False)
    own_rows(6, True)

    ring_step(7)
    for way, n in ((0, 0), (1, 1), (1, 2), (0, 3)):
        share(*f_got(way, n))
    own_rows(6, False)
    own_rows(7, True)
    for n in range(12, 16):
        build_col(sibling[n])
        build_col(share_got(n))
    own_rows(7, False)
    product(0, True)

    ring_step(8)
    own_rows(8, True)
    far_rows(0)
    product(0, False)
    own_rows(8, False)
    product(1, True)
    far_rows(1)
    product(1, False)

    for copy in started:
        copy.wait_send()
    for t in range(HALF + 1):
        for slot, panel in slots(t):
            hand(slot, panel, False)


def on_device(amplitude, spectrum, freq_index, star_offsets, valid_mask):
    width = amplitude.shape[1]
    vmem = pl.BlockSpec(memory_space=pltpu.VMEM)
    dma = pltpu.SemaphoreType.DMA
    return pl.pallas_call(
        kernel,
        out_shape=jax.ShapeDtypeStruct((1, 4 * PANEL, 2 * NX * PANEL), jnp.bfloat16),
        in_specs=[vmem, vmem, vmem, pl.BlockSpec(memory_space=pltpu.SMEM), vmem],
        out_specs=vmem,
        scratch_shapes=[
            pltpu.VMEM((NZ, 4, PANEL, width), jnp.bfloat16),
            pltpu.VMEM((4, 2 * NX, PANEL, width), jnp.bfloat16),
            pltpu.VMEM((2, 4 * PANEL, 4 * width), jnp.bfloat16),
            pltpu.VMEM((2, 2 * NX * PANEL, 4 * width), jnp.bfloat16),
            pltpu.VMEM((4, 8, width), jnp.float32),
            pltpu.VMEM((4, PANEL, width), jnp.float32),
            pltpu.VMEM((4, PANEL, width), jnp.float32),
            pltpu.VMEM((24, width), jnp.float32),
            pltpu.VMEM((4, 24, width), jnp.float32),
            pltpu.VMEM((4, 24, width), jnp.float32),
            pltpu.VMEM((PANEL, PANEL), jnp.float32),
            pltpu.VMEM((4 * PANEL, 2 * NX * PANEL), jnp.float32),
            dma((2, HALF, SUBS)), dma((2, HALF, SUBS)),
            dma((16,)), dma((4, 4)),
            dma((3,)), dma((3,)),
            dma((3,)), dma((3,)),
            dma((2, 4)), dma((2, 4)),
            dma((2, 2)), dma((2, 2)),
            dma((16,)), dma((16,)),
        ],
        compiler_params=pltpu.CompilerParams(
            collective_id=0, has_side_effects=True, vmem_limit_bytes=36 * 2**20
        ),
        cost_estimate=pl.CostEstimate(flops=2 * 512 * 1024 * 4096, bytes_accessed=2 * 2**20, transcendentals=0),
    )(amplitude, spectrum.reshape(1, width), freq_index, star_offsets.T, valid_mask.reshape(1, PANEL))


def solution(mesh):
    placed = (P("grid", "freq"), P("freq"), P(None, "freq"), P(), P("grid"))
    return jax.shard_map(
        on_device, mesh=mesh, in_specs=placed, out_specs=P("grid", "freq", None), check_vma=False
    )
```

```python
import math

import jax
import jax.numpy as jnp
from jax import lax
from jax.experimental import pallas as pl
from jax.experimental.pallas import tpu as pltpu
from jax.sharding import PartitionSpec as P

NGS = 9
PANEL = 128
NZ = 16
NX = 4
SUBS = 4
HALF = NZ // 2
MESH = pl.DeviceIdType.MESH


def cos_sin(phase):
    index = phase.astype(jnp.int32) & 511
    quadrant = (index + 64) >> 7
    x = (index - (quadrant << 7)).astype(jnp.float32) * (2.0 * math.pi / 512.0)
    y = x * x
    sin = x * (1.0 + y * (-1 / 6 + y * (1 / 120 + y * (-1 / 5040 + y * (1 / 362880)))))
    cos = 1.0 + y * (-0.5 + y * (1 / 24 + y * (-1 / 720 + y * (1 / 40320 + y * (-1 / 3628800)))))
    swap = (quadrant & 1) == 1
    cos, sin = jnp.where(swap, sin, cos), jnp.where(swap, cos, sin)
    cos = jnp.where(((quadrant + 1) & 2) != 0, -cos, cos)
    sin = jnp.where((quadrant & 2) != 0, -sin, sin)
    return cos, sin


def kernel(
    amp_ref, spec_ref, freq_ref, star_ref, mask_ref, out_ref,
    rows, cols, rop, cop, pack, base_c, base_s, turn_p, turn_c, turn_s, mask_t, acc,
    zs, zr, hs, hr, ps, pr, ys, yr, xs, xr, fs, fr, ss, sr,
):
    g, f = lax.axis_index("grid"), lax.axis_index("freq")
    z, a = g % NZ, g // NZ
    x, yh = a // 2, a % 2
    yl, core = f // 2, f % 2
    width = amp_ref.shape[1]

    f1 = f + 1 - 2 * core
    f2 = f + 2 - 4 * yl
    f3 = f1 + 2 - 4 * yl
    a_far = a + 1 - 2 * yh
    g_far = a_far * NZ + z

    def at_z(step):
        return a * NZ + (z + step + NZ) % NZ

    def at_x(step):
        return (((x + step + NX) % NX) * 2 + yh) * NZ + z

    barrier = pltpu.get_barrier_semaphore()
    peers = [
        (at_z(1), f), (at_z(-1), f), (g, f1), (g, f2), (g, f3),
        (g_far, f), (g_far, f2), (at_x(1), f), (at_x(-1), f),
    ]
    for peer in peers:
        pl.semaphore_signal(barrier, inc=1, device_id=peer, device_id_type=MESH)

    mask_t[...] = jnp.broadcast_to(mask_ref[...].astype(jnp.float32), (PANEL, PANEL)).T
    for n in range(width // 128):
        lanes = pl.ds(n * 128, 128)
        masked = (amp_ref[:, lanes].astype(jnp.float32) * mask_t[...]).astype(jnp.bfloat16)
        rows[z, f, :, lanes] = masked
        cols[f, a, :, lanes] = masked
    total = width * lax.axis_size("freq")
    pack[f, 0:2, :] = freq_ref[...].astype(jnp.float32)
    pack[f, 2:3, :] = jnp.sqrt(spec_ref[...] / total)

    pl.semaphore_wait(barrier, len(peers))

    started = []

    def send(src, dst, send_sem, recv_sem, peer):
        return pltpu.make_async_remote_copy(
            src_ref=src, dst_ref=dst, send_sem=send_sem, recv_sem=recv_sem,
            device_id=peer, device_id_type=MESH,
        )

    def begin(copy):
        copy.start()
        started.append(copy)

    piece = PANEL // SUBS

    def ring(t, way, sub):
        panel = (z - (1, -1)[way] * (t - 1) + NZ) % NZ
        part = rows.at[panel, f, pl.ds(sub * piece, piece)]
        return send(part, part, zs.at[way, t - 1, sub], zr.at[way, t - 1, sub], (at_z((1, -1)[way]), f))

    def ring_got(t, way, sub):
        panel = (z - (1, -1)[way] * t + NZ) % NZ
        part = rows.at[panel, f, pl.ds(sub * piece, piece)]
        send(part, part, zs.at[way, t - 1, sub], zr.at[way, t - 1, sub], (at_z((1, -1)[way]), f)).wait_recv()

    def ways(t, sub):
        if t < HALF:
            return (0, 1)
        return (0,) if sub < SUBS // 2 else (1,)

    def hand(slot, panel, start):
        owner, place = panel // 4, panel % 4

        @pl.when(owner != f)
        def _():
            copy = send(rows.at[panel, f], rows.at[panel, f], hs.at[slot], hr.at[place, f], (g, owner))
            if start:
                copy.start()
            else:
                copy.wait_send()

    def slots(t):
        if t == 0:
            return [(0, z)]
        if t == HALF:
            return [(2 * HALF - 1, (z + HALF) % NZ)]
        return [(2 * t - 1, (z - t + NZ) % NZ), (2 * t, (z + t) % NZ)]

    def ring_step(t):
        for sub in range(SUBS):
            for way in ways(t, sub):
                ring_got(t, way, sub)
                if t < HALF and way in ways(t + 1, sub):
                    begin(ring(t + 1, way, sub))
        for slot, panel in slots(t):
            hand(slot, panel, True)

    def col_send(panel, q, send_sem, recv_sem, peer):
        return send(cols.at[q, panel], cols.at[q, panel], send_sem, recv_sem, peer)

    def y_copies():
        return [
            col_send(a, f, ys.at[0], yr.at[0], (g_far, f2)),
            col_send(a, f, ys.at[1], yr.at[1], (g, f2)),
            col_send(a, f, ys.at[2], yr.at[2], (g_far, f)),
        ]

    y_items = [(a_far, f2), (a, f2), (a_far, f)]
    quad = [(0, f), (1, f2), (0, f2), (1, f)]

    def col_of(step, other):
        return ((x + step + NX) % NX) * 2 + (yh if other == 0 else 1 - yh)

    def x_copy(n, way):
        other, q = quad[n]
        return col_send(col_of(0, other), q, xs.at[way, n], xr.at[way, n], (at_x((1, -1)[way]), f))

    def x_got(n, way):
        other, q = quad[n]
        panel = col_of(-(1, -1)[way], other)
        col_send(panel, q, xs.at[way, n], xr.at[way, n], (at_x(0), f)).wait_recv()
        return panel, q

    forward = {(0, 0): 0, (0, 3): 1, (1, 1): 0, (1, 2): 1}

    def x_forward(n, way):
        other, q = quad[n]
        panel = col_of(-(1, -1)[way], other)
        return col_send(panel, q, fs.at[way, forward[way, n]], fr.at[way, forward[way, n]], (at_x((1, -1)[way]), f))

    def f_got(way, n):
        other, q = quad[n]
        panel = col_of(2, other)
        col_send(panel, q, fs.at[way, forward[way, n]], fr.at[way, forward[way, n]], (at_x(0), f)).wait_recv()
        return panel, q

    sibling = []

    def share(panel, q):
        n = len(sibling)
        sibling.append((panel, q))
        begin(col_send(panel, q, ss.at[n], sr.at[n], (g, f1)))

    def other_core(q):
        return q + 1 - 2 * core

    def share_got(n):
        panel, q = sibling[n]
        mine = other_core(q)
        col_send(panel, mine, ss.at[n], sr.at[n], (g, f1)).wait_recv()
        return panel, mine

    def base_table(q):
        kx = pack[q, 0:1, :]

        def step(i, carry):
            at = pl.ds(pl.multiple_of(i * 16, 16), 16)
            across = (lax.broadcasted_iota(jnp.int32, (16, width), 0) + i * 16) >> 1
            cos, sin = cos_sin(kx * (2 * across).astype(jnp.float32))
            base_c[q, at, :] = cos
            base_s[q, at, :] = sin
            return carry

        lax.fori_loop(0, PANEL // 16, step, 0)

    slope_count = PANEL * lax.axis_size("grid")
    group = a * NZ + f * 4
    turn_panels = [n * NZ + z for n in range(2 * NX)] + [group + n for n in range(4)]

    def turn_table(q):
        kx, ky = pack[q, 0:1, :], pack[q, 1:2, :]
        for n, panel in enumerate(turn_panels):
            upward = 2 * (panel % 64)
            star = panel * PANEL * NGS // slope_count
            for m in range(2):
                index = jnp.minimum(star + m, NGS - 1)
                turn_x = star_ref[0, index].astype(jnp.float32)
                turn_y = (star_ref[1, index] + upward).astype(jnp.float32)
                turn_p[2 * n + m : 2 * n + m + 1, :] = kx * turn_x + ky * turn_y
        weight = pack[q, 2:3, :]
        cos, sin = cos_sin(turn_p[...])
        turn_c[q] = cos * weight
        turn_s[q] = sin * weight

    def build(source, panel, q, turn, into):
        star = panel * PANEL * NGS // slope_count
        bound = ((star + 1) * slope_count + NGS - 1) // NGS - panel * PANEL
        c0, c1 = turn_c[q, pl.ds(2 * turn, 1), :], turn_c[q, pl.ds(2 * turn + 1, 1), :]
        s0, s1 = turn_s[q, pl.ds(2 * turn, 1), :], turn_s[q, pl.ds(2 * turn + 1, 1), :]

        def step(i, carry):
            at = pl.ds(pl.multiple_of(i * 16, 16), 16)
            first = lax.broadcasted_iota(jnp.int32, (16, width), 0) + i * 16 < bound
            tc, ts = jnp.where(first, c0, c1), jnp.where(first, s0, s1)
            value = source[at, :].astype(jnp.float32)
            bc, bs = base_c[q, at, :], base_s[q, at, :]
            into(i, (value * (bc * tc - bs * ts)).astype(jnp.bfloat16), (value * (bs * tc + bc * ts)).astype(jnp.bfloat16))
            return carry

        lax.fori_loop(0, PANEL // 16, step, 0, unroll=8)

    def build_col(item):
        panel, q = item
        half, part = q // 2, q % 2

        def into(i, cos, sin):
            at = pl.ds(pl.multiple_of(panel * PANEL + i * 16, 16), 16)
            cop[half, at, pl.ds(pl.multiple_of(part * 2 * width, 128), width)] = cos
            cop[half, at, pl.ds(pl.multiple_of(part * 2 * width + width, 128), width)] = sin

        build(cols.at[q, panel], panel * NZ + z, q, panel, into)

    ahead = (4 * f + 1 - z + NZ) % NZ < HALF

    def row_operand(place, q):
        panel = 4 * f + place
        part = q % 2

        def into(i, cos, sin):
            at = pl.ds(pl.multiple_of(place * PANEL + i * 16, 16), 16)
            rop[q // 2, at, pl.ds(pl.multiple_of(part * 2 * width, 128), width)] = cos
            rop[q // 2, at, pl.ds(pl.multiple_of(part * 2 * width + width, 128), width)] = sin

        build(rows.at[panel, q], a * NZ + panel, q, 2 * NX + place, into)

    def handed(place, q):
        part = rows.at[4 * f + place, q]
        send(part, part, hs.at[0], hr.at[place, q], (g, f1)).wait_recv()
        row_operand(place, q)

    def own_rows(t, of_core):
        for _, panel in slots(t):
            @pl.when(panel // 4 == f)
            def _():
                if of_core:
                    row_operand(panel % 4, f)
                else:
                    handed(panel % 4, f1)

    def product(m, near):
        half = yl if near else 1 - yl
        at = pl.ds(pl.multiple_of(jnp.where(ahead, 2 * m, 2 - 2 * m) * PANEL, PANEL), 2 * PANEL)

        def dot(i, carry):
            to = pl.ds(pl.multiple_of(i * 1024, 1024), 1024)
            value = lax.dot_general(
                rop[half, at, :], cop[half, to, :], (((1,), (1,)), ((), ())), preferred_element_type=jnp.float32
            )
            if near:
                acc[at, to] = value
            else:
                out_ref[0, at, to] = (acc[at, to] + value).astype(jnp.bfloat16)
            return carry

        lax.fori_loop(0, cop.shape[1] // 1024, dot, 0)

    def far_rows(m):
        for n in range(2):
            for q in (f2, f3):
                handed(jnp.where(ahead, 2 * m + n, 3 - 2 * m - n), q)

    for sub in range(SUBS):
        for way in (0, 1):
            begin(ring(1, way, sub))
    packs = [
        send(pack.at[f], pack.at[f], ps.at[n], pr.at[n], (g, peer)) for n, peer in enumerate((f1, f2, f3))
    ]
    for copy in packs:
        begin(copy)
    for copy in y_copies():
        begin(copy)
    for way in (0, 1):
        begin(x_copy(0, way))
    hand(0, z, True)
    share(a, f)

    base_table(f)
    turn_table(f)
    for n, q in enumerate((f1, f2, f3)):
        send(pack.at[q], pack.at[q], ps.at[n], pr.at[n], (g, q)).wait_recv()
        if n == 0:
            base_table(q)
            turn_table(q)

    own_rows(0, True)
    def y_step(n):
        panel, q = y_items[n]
        col_send(panel, q, ys.at[n], yr.at[n], (g, f)).wait_recv()
        for way in (0, 1):
            begin(x_copy(n + 1, way))
        share(panel, q)

    def x_step(n):
        for way in (0, 1):
            item = x_got(n, way)
            if (way, n) in forward:
                begin(x_forward(n, way))
            share(*item)

    def both_cols(*numbers):
        for n in numbers:
            build_col(sibling[n])
            build_col(share_got(n))

    ring_step(1)
    base_table(f2)
    turn_table(f2)
    base_table(f3)
    turn_table(f3)
    own_rows(0, False)
    own_rows(1, True)
    y_step(0)
    y_step(1)

    ring_step(2)
    y_step(2)
    x_step(0)
    both_cols(0)
    own_rows(1, False)
    own_rows(2, True)

    ring_step(3)
    both_cols(1, 2, 3)
    own_rows(2, False)
    own_rows(3, True)
    x_step(1)

    ring_step(4)
    x_step(2)
    both_cols(4, 5)
    own_rows(3, False)
    own_rows(4, True)

    ring_step(5)
    x_step(3)
    share(*f_got(0, 0))
    both_cols(6, 7, 8, 9)
    own_rows(4, False)
    own_rows(5, True)

    ring_step(6)
    share(*f_got(1, 1))
    share(*f_got(1, 2))
    both_cols(10, 11, 12)
    own_rows(5, False)
    own_rows(6, True)
    both_cols(13)

    ring_step(7)
    share(*f_got(0, 3))
    own_rows(6, False)
    own_rows(7, True)
    both_cols(14, 15)
    own_rows(7, False)
    product(0, True)

    ring_step(8)
    own_rows(8, True)
    own_rows(8, False)
    product(1, True)
    far_rows(0)
    product(0, False)
    far_rows(1)
    product(1, False)

    for copy in started:
        copy.wait_send()
    for t in range(HALF + 1):
        for slot, panel in slots(t):
            hand(slot, panel, False)


def on_device(amplitude, spectrum, freq_index, star_offsets, valid_mask):
    width = amplitude.shape[1]
    vmem = pl.BlockSpec(memory_space=pltpu.VMEM)
    dma = pltpu.SemaphoreType.DMA
    return pl.pallas_call(
        kernel,
        out_shape=jax.ShapeDtypeStruct((1, 4 * PANEL, 2 * NX * PANEL), jnp.bfloat16),
        in_specs=[vmem, vmem, vmem, pl.BlockSpec(memory_space=pltpu.SMEM), vmem],
        out_specs=vmem,
        scratch_shapes=[
            pltpu.VMEM((NZ, 4, PANEL, width), jnp.bfloat16),
            pltpu.VMEM((4, 2 * NX, PANEL, width), jnp.bfloat16),
            pltpu.VMEM((2, 4 * PANEL, 4 * width), jnp.bfloat16),
            pltpu.VMEM((2, 2 * NX * PANEL, 4 * width), jnp.bfloat16),
            pltpu.VMEM((4, 8, width), jnp.float32),
            pltpu.VMEM((4, PANEL, width), jnp.float32),
            pltpu.VMEM((4, PANEL, width), jnp.float32),
            pltpu.VMEM((24, width), jnp.float32),
            pltpu.VMEM((4, 24, width), jnp.float32),
            pltpu.VMEM((4, 24, width), jnp.float32),
            pltpu.VMEM((PANEL, PANEL), jnp.float32),
            pltpu.VMEM((4 * PANEL, 2 * NX * PANEL), jnp.float32),
            dma((2, HALF, SUBS)), dma((2, HALF, SUBS)),
            dma((16,)), dma((4, 4)),
            dma((3,)), dma((3,)),
            dma((3,)), dma((3,)),
            dma((2, 4)), dma((2, 4)),
            dma((2, 2)), dma((2, 2)),
            dma((16,)), dma((16,)),
        ],
        compiler_params=pltpu.CompilerParams(
            collective_id=0, has_side_effects=True, vmem_limit_bytes=36 * 2**20
        ),
        cost_estimate=pl.CostEstimate(flops=2 * 512 * 1024 * 4096, bytes_accessed=2 * 2**20, transcendentals=0),
    )(amplitude, spectrum.reshape(1, width), freq_index, star_offsets.T, valid_mask.reshape(1, PANEL))


def solution(mesh):
    placed = (P("grid", "freq"), P("freq"), P(None, "freq"), P(), P("grid"))
    return jax.shard_map(
        on_device, mesh=mesh, in_specs=placed, out_specs=P("grid", "freq", None), check_vma=False
    )
```

```python
import math

import jax
import jax.numpy as jnp
from jax import lax
from jax.experimental import pallas as pl
from jax.experimental.pallas import tpu as pltpu
from jax.sharding import PartitionSpec as P

NGS = 9
PANEL = 128
NZ = 16
NX = 4
SUBS = 4
HALF = NZ // 2
MESH = pl.DeviceIdType.MESH


def cos_sin(phase):
    index = phase.astype(jnp.int32) & 511
    quadrant = (index + 64) >> 7
    x = (index - (quadrant << 7)).astype(jnp.float32) * (2.0 * math.pi / 512.0)
    y = x * x
    sin = x * (1.0 + y * (-1 / 6 + y * (1 / 120 + y * (-1 / 5040 + y * (1 / 362880)))))
    cos = 1.0 + y * (-0.5 + y * (1 / 24 + y * (-1 / 720 + y * (1 / 40320 + y * (-1 / 3628800)))))
    swap = (quadrant & 1) == 1
    cos, sin = jnp.where(swap, sin, cos), jnp.where(swap, cos, sin)
    cos = jnp.where(((quadrant + 1) & 2) != 0, -cos, cos)
    sin = jnp.where((quadrant & 2) != 0, -sin, sin)
    return cos, sin


def kernel(
    amp_ref, spec_ref, freq_ref, star_ref, out_ref,
    rows, cols, rop, cop, pack, base_c, base_s, turn_p, turn_c, turn_s, acc,
    zs, zr, hs, hr, ps, pr, ys, yr, xs, xr, fs, fr, ss, sr,
):
    g, f = lax.axis_index("grid"), lax.axis_index("freq")
    z, a = g % NZ, g // NZ
    x, yh = a // 2, a % 2
    yl, core = f // 2, f % 2
    width = amp_ref.shape[1]

    f1 = f + 1 - 2 * core
    f2 = f + 2 - 4 * yl
    f3 = f1 + 2 - 4 * yl
    a_far = a + 1 - 2 * yh
    g_far = a_far * NZ + z

    def at_z(step):
        return a * NZ + (z + step + NZ) % NZ

    def at_x(step):
        return (((x + step + NX) % NX) * 2 + yh) * NZ + z

    barrier = pltpu.get_barrier_semaphore()
    peers = [
        (at_z(1), f), (at_z(-1), f), (g, f1), (g, f2), (g, f3),
        (g_far, f), (g_far, f2), (at_x(1), f), (at_x(-1), f),
    ]
    for peer in peers:
        pl.semaphore_signal(barrier, inc=1, device_id=peer, device_id_type=MESH)

    rows[z, f] = amp_ref[...]
    cols[f, a] = amp_ref[...]
    total = width * lax.axis_size("freq")
    pack[f, 0:2, :] = freq_ref[...].astype(jnp.float32)
    pack[f, 2:3, :] = jnp.sqrt(spec_ref[...] / total)

    pl.semaphore_wait(barrier, len(peers))

    started = []

    def send(src, dst, send_sem, recv_sem, peer):
        return pltpu.make_async_remote_copy(
            src_ref=src, dst_ref=dst, send_sem=send_sem, recv_sem=recv_sem,
            device_id=peer, device_id_type=MESH,
        )

    def begin(copy):
        copy.start()
        started.append(copy)

    piece = PANEL // SUBS

    def ring(t, way, sub):
        panel = (z - (1, -1)[way] * (t - 1) + NZ) % NZ
        part = rows.at[panel, f, pl.ds(sub * piece, piece)]
        return send(part, part, zs.at[way, t - 1, sub], zr.at[way, t - 1, sub], (at_z((1, -1)[way]), f))

    def ring_got(t, way, sub):
        panel = (z - (1, -1)[way] * t + NZ) % NZ
        part = rows.at[panel, f, pl.ds(sub * piece, piece)]
        send(part, part, zs.at[way, t - 1, sub], zr.at[way, t - 1, sub], (at_z((1, -1)[way]), f)).wait_recv()

    def ways(t, sub):
        if t < HALF:
            return (0, 1)
        return (0,) if sub < SUBS // 2 else (1,)

    def hand(slot, panel, start):
        owner, place = panel // 4, panel % 4

        @pl.when(owner != f)
        def _():
            copy = send(rows.at[panel, f], rows.at[panel, f], hs.at[slot], hr.at[place, f], (g, owner))
            if start:
                copy.start()
            else:
                copy.wait_send()

    def slots(t):
        if t == 0:
            return [(0, z)]
        if t == HALF:
            return [(2 * HALF - 1, (z + HALF) % NZ)]
        return [(2 * t - 1, (z - t + NZ) % NZ), (2 * t, (z + t) % NZ)]

    def ring_step(t):
        for sub in range(SUBS):
            for way in ways(t, sub):
                ring_got(t, way, sub)
                if t < HALF and way in ways(t + 1, sub):
                    begin(ring(t + 1, way, sub))
        for slot, panel in slots(t):
            hand(slot, panel, True)

    def col_send(panel, q, send_sem, recv_sem, peer):
        return send(cols.at[q, panel], cols.at[q, panel], send_sem, recv_sem, peer)

    def y_copies():
        return [
            col_send(a, f, ys.at[0], yr.at[0], (g_far, f2)),
            col_send(a, f, ys.at[1], yr.at[1], (g, f2)),
            col_send(a, f, ys.at[2], yr.at[2], (g_far, f)),
        ]

    y_items = [(a_far, f2), (a, f2), (a_far, f)]
    quad = [(0, f), (1, f2), (0, f2), (1, f)]

    def col_of(step, other):
        return ((x + step + NX) % NX) * 2 + (yh if other == 0 else 1 - yh)

    def x_copy(n, way):
        other, q = quad[n]
        return col_send(col_of(0, other), q, xs.at[way, n], xr.at[way, n], (at_x((1, -1)[way]), f))

    def x_got(n, way):
        other, q = quad[n]
        panel = col_of(-(1, -1)[way], other)
        col_send(panel, q, xs.at[way, n], xr.at[way, n], (at_x(0), f)).wait_recv()
        return panel, q

    forward = {(0, 0): 0, (0, 3): 1, (1, 1): 0, (1, 2): 1}

    def x_forward(n, way):
        other, q = quad[n]
        panel = col_of(-(1, -1)[way], other)
        return col_send(panel, q, fs.at[way, forward[way, n]], fr.at[way, forward[way, n]], (at_x((1, -1)[way]), f))

    def f_got(way, n):
        other, q = quad[n]
        panel = col_of(2, other)
        col_send(panel, q, fs.at[way, forward[way, n]], fr.at[way, forward[way, n]], (at_x(0), f)).wait_recv()
        return panel, q

    sibling = []

    def share(panel, q):
        n = len(sibling)
        sibling.append((panel, q))
        begin(col_send(panel, q, ss.at[n], sr.at[n], (g, f1)))

    def other_core(q):
        return q + 1 - 2 * core

    def share_got(n):
        panel, q = sibling[n]
        mine = other_core(q)
        col_send(panel, mine, ss.at[n], sr.at[n], (g, f1)).wait_recv()
        return panel, mine

    def base_table(q):
        kx = pack[q, 0:1, :]

        def step(i, carry):
            at = pl.ds(pl.multiple_of(i * 16, 16), 16)
            across = (lax.broadcasted_iota(jnp.int32, (16, width), 0) + i * 16) >> 1
            cos, sin = cos_sin(kx * (2 * across).astype(jnp.float32))
            base_c[q, at, :] = cos
            base_s[q, at, :] = sin
            return carry

        lax.fori_loop(0, PANEL // 16, step, 0)

    slope_count = PANEL * lax.axis_size("grid")
    group = a * NZ + f * 4
    turn_panels = [n * NZ + z for n in range(2 * NX)] + [group + n for n in range(4)]

    def turn_table(q):
        kx, ky = pack[q, 0:1, :], pack[q, 1:2, :]
        for n, panel in enumerate(turn_panels):
            upward = 2 * (panel % 64)
            star = panel * PANEL * NGS // slope_count
            for m in range(2):
                index = jnp.minimum(star + m, NGS - 1)
                turn_x = star_ref[0, index].astype(jnp.float32)
                turn_y = (star_ref[1, index] + upward).astype(jnp.float32)
                turn_p[2 * n + m : 2 * n + m + 1, :] = kx * turn_x + ky * turn_y
        weight = pack[q, 2:3, :]
        cos, sin = cos_sin(turn_p[...])
        turn_c[q] = cos * weight
        turn_s[q] = sin * weight

    def build(source, panel, q, turn, into):
        star = panel * PANEL * NGS // slope_count
        bound = ((star + 1) * slope_count + NGS - 1) // NGS - panel * PANEL
        c0, c1 = turn_c[q, pl.ds(2 * turn, 1), :], turn_c[q, pl.ds(2 * turn + 1, 1), :]
        s0, s1 = turn_s[q, pl.ds(2 * turn, 1), :], turn_s[q, pl.ds(2 * turn + 1, 1), :]

        def step(i, carry):
            at = pl.ds(pl.multiple_of(i * 16, 16), 16)
            first = lax.broadcasted_iota(jnp.int32, (16, width), 0) + i * 16 < bound
            tc, ts = jnp.where(first, c0, c1), jnp.where(first, s0, s1)
            value = source[at, :].astype(jnp.float32)
            bc, bs = base_c[q, at, :], base_s[q, at, :]
            into(i, (value * (bc * tc - bs * ts)).astype(jnp.bfloat16), (value * (bs * tc + bc * ts)).astype(jnp.bfloat16))
            return carry

        lax.fori_loop(0, PANEL // 16, step, 0, unroll=8)

    def build_col(item):
        panel, q = item
        half, part = q // 2, q % 2

        def into(i, cos, sin):
            at = pl.ds(pl.multiple_of(panel * PANEL + i * 16, 16), 16)
            cop[half, at, pl.ds(pl.multiple_of(part * 2 * width, 128), width)] = cos
            cop[half, at, pl.ds(pl.multiple_of(part * 2 * width + width, 128), width)] = sin

        build(cols.at[q, panel], panel * NZ + z, q, panel, into)

    ahead = (4 * f + 1 - z + NZ) % NZ < HALF

    def row_operand(place, q):
        panel = 4 * f + place
        part = q % 2

        def into(i, cos, sin):
            at = pl.ds(pl.multiple_of(place * PANEL + i * 16, 16), 16)
            rop[q // 2, at, pl.ds(pl.multiple_of(part * 2 * width, 128), width)] = cos
            rop[q // 2, at, pl.ds(pl.multiple_of(part * 2 * width + width, 128), width)] = sin

        build(rows.at[panel, q], a * NZ + panel, q, 2 * NX + place, into)

    def handed(place, q):
        part = rows.at[4 * f + place, q]
        send(part, part, hs.at[0], hr.at[place, q], (g, f1)).wait_recv()
        row_operand(place, q)

    def own_rows(t, of_core):
        for _, panel in slots(t):
            @pl.when(panel // 4 == f)
            def _():
                if of_core:
                    row_operand(panel % 4, f)
                else:
                    handed(panel % 4, f1)

    def product(m, near):
        half = yl if near else 1 - yl
        at = pl.ds(pl.multiple_of(jnp.where(ahead, 2 * m, 2 - 2 * m) * PANEL, PANEL), 2 * PANEL)

        def dot(i, carry):
            to = pl.ds(pl.multiple_of(i * 1024, 1024), 1024)
            value = lax.dot_general(
                rop[half, at, :], cop[half, to, :], (((1,), (1,)), ((), ())), preferred_element_type=jnp.float32
            )
            if near:
                acc[at, to] = value
            else:
                out_ref[0, at, to] = (acc[at, to] + value).astype(jnp.bfloat16)
            return carry

        lax.fori_loop(0, cop.shape[1] // 1024, dot, 0)

    def far_rows(m):
        for n in range(2):
            for q in (f2, f3):
                handed(jnp.where(ahead, 2 * m + n, 3 - 2 * m - n), q)

    for sub in range(SUBS):
        for way in (0, 1):
            begin(ring(1, way, sub))
    packs = [
        send(pack.at[f], pack.at[f], ps.at[n], pr.at[n], (g, peer)) for n, peer in enumerate((f1, f2, f3))
    ]
    for copy in packs:
        begin(copy)
    for copy in y_copies():
        begin(copy)
    for way in (0, 1):
        begin(x_copy(0, way))
    hand(0, z, True)
    share(a, f)

    base_table(f)
    turn_table(f)
    for n, q in enumerate((f1, f2, f3)):
        send(pack.at[q], pack.at[q], ps.at[n], pr.at[n], (g, q)).wait_recv()
        if n == 0:
            base_table(q)
            turn_table(q)

    own_rows(0, True)
    def y_step(n):
        panel, q = y_items[n]
        col_send(panel, q, ys.at[n], yr.at[n], (g, f)).wait_recv()
        for way in (0, 1):
            begin(x_copy(n + 1, way))
        share(panel, q)

    def x_step(n):
        for way in (0, 1):
            item = x_got(n, way)
            if (way, n) in forward:
                begin(x_forward(n, way))
            share(*item)

    def both_cols(*numbers):
        for n in numbers:
            build_col(sibling[n])
            build_col(share_got(n))

    ring_step(1)
    base_table(f2)
    turn_table(f2)
    base_table(f3)
    turn_table(f3)
    own_rows(0, False)
    own_rows(1, True)
    y_step(0)
    y_step(1)

    ring_step(2)
    y_step(2)
    x_step(0)
    both_cols(0)
    own_rows(1, False)
    own_rows(2, True)

    ring_step(3)
    both_cols(1, 2, 3)
    own_rows(2, False)
    own_rows(3, True)
    x_step(1)

    ring_step(4)
    x_step(2)
    both_cols(4, 5)
    own_rows(3, False)
    own_rows(4, True)

    ring_step(5)
    x_step(3)
    share(*f_got(0, 0))
    both_cols(6, 7, 8, 9)
    own_rows(4, False)
    own_rows(5, True)

    ring_step(6)
    share(*f_got(1, 1))
    share(*f_got(1, 2))
    both_cols(10, 11, 12)
    own_rows(5, False)
    own_rows(6, True)
    both_cols(13)

    ring_step(7)
    share(*f_got(0, 3))
    own_rows(6, False)
    own_rows(7, True)
    both_cols(14, 15)
    own_rows(7, False)
    product(0, True)

    ring_step(8)
    own_rows(8, True)
    own_rows(8, False)
    product(1, True)
    far_rows(0)
    product(0, False)
    far_rows(1)
    product(1, False)

    for copy in started:
        copy.wait_send()
    for t in range(HALF + 1):
        for slot, panel in slots(t):
            hand(slot, panel, False)


def on_device(amplitude, spectrum, freq_index, star_offsets, valid_mask):
    width = amplitude.shape[1]
    masked = amplitude * valid_mask.astype(jnp.bfloat16)[:, None]
    vmem = pl.BlockSpec(memory_space=pltpu.VMEM)
    dma = pltpu.SemaphoreType.DMA
    return pl.pallas_call(
        kernel,
        out_shape=jax.ShapeDtypeStruct((1, 4 * PANEL, 2 * NX * PANEL), jnp.bfloat16),
        in_specs=[vmem, vmem, vmem, pl.BlockSpec(memory_space=pltpu.SMEM)],
        out_specs=vmem,
        scratch_shapes=[
            pltpu.VMEM((NZ, 4, PANEL, width), jnp.bfloat16),
            pltpu.VMEM((4, 2 * NX, PANEL, width), jnp.bfloat16),
            pltpu.VMEM((2, 4 * PANEL, 4 * width), jnp.bfloat16),
            pltpu.VMEM((2, 2 * NX * PANEL, 4 * width), jnp.bfloat16),
            pltpu.VMEM((4, 8, width), jnp.float32),
            pltpu.VMEM((4, PANEL, width), jnp.float32),
            pltpu.VMEM((4, PANEL, width), jnp.float32),
            pltpu.VMEM((24, width), jnp.float32),
            pltpu.VMEM((4, 24, width), jnp.float32),
            pltpu.VMEM((4, 24, width), jnp.float32),
            pltpu.VMEM((4 * PANEL, 2 * NX * PANEL), jnp.float32),
            dma((2, HALF, SUBS)), dma((2, HALF, SUBS)),
            dma((16,)), dma((4, 4)),
            dma((3,)), dma((3,)),
            dma((3,)), dma((3,)),
            dma((2, 4)), dma((2, 4)),
            dma((2, 2)), dma((2, 2)),
            dma((16,)), dma((16,)),
        ],
        compiler_params=pltpu.CompilerParams(
            collective_id=0, has_side_effects=True, vmem_limit_bytes=36 * 2**20
        ),
        cost_estimate=pl.CostEstimate(flops=2 * 512 * 1024 * 4096, bytes_accessed=2 * 2**20, transcendentals=0),
    )(masked, spectrum.reshape(1, width), freq_index, star_offsets.T)


def solution(mesh):
    placed = (P("grid", "freq"), P("freq"), P(None, "freq"), P(), P("grid"))
    return jax.shard_map(
        on_device, mesh=mesh, in_specs=placed, out_specs=P("grid", "freq", None), check_vma=False
    )
```
